512 devices in a mesh: seq: 64 (over y, x, core), chan: 8 (over z).
Axes of the slice: x: 4, y: 8, z: 8, core: 2. Of those that a mesh axis runs over, the one named last changes fastest.
Arguments:
- hidden_in: bfloat16 [8192, 8192], P('seq', 'chan'), as said below
- query_mr: bfloat16 [8192, 8192], P('seq', 'chan'), may hold values from -6 to 6
- key_mr: bfloat16 [8192, 8192], P('seq', 'chan'), may hold values from -6 to 6
- value_mr: bfloat16 [8192, 8192], P('seq', 'chan'), may hold values from -6 to 6
- query_li: bfloat16 [8192, 8192], P('seq', 'chan'), may hold values from -6 to 6
- key_li: bfloat16 [8192, 8192], P('seq', 'chan'), may hold values from -6 to 6
- mr_filter: bfloat16 [128, 512], P(None, 'chan'), may hold values from -0.5 to 0.5
- li_rate: float32 [16, 8192], P(None, 'chan'), as said below
- li_residue: float32 [16, 8192], P(None, 'chan'), may hold values from -4 to 4
- norm_gain: float32 [8192], P('chan'), may hold values from 0.25 to 1.75
Outputs:
- normed_out: bfloat16 [8192, 8192], P('seq', 'chan')
The draws below stay inside these ranges and needn't reach their ends.
Inputs may be any that keep to these rules, and one draw needn't show every extreme that they name: `hidden_in`: real values of moderate size. `li_rate`: decay rates per position, all positive, from 1 / 81920 to 1 / 30.
All inputs are finite; a program needn't handle non-finite values.
Results may differ from the reference program's by a relative error of at most 0.0055.
Values may be sent and summed in bfloat16 or wider, within the bound.
No kernel may reach another device: no remote copies, remote signals or barrier semaphores. Data moves between devices by JAX's collectives and lax.ppermute only.
A program may use at most 64 MiB of HBM per device.

```python
import math
import jax
import jax.numpy as jnp
from jax import lax

D = 8192
MR_LEN = 128
POLES = 16
TOKENS = 8192
MR_GROUPS = 512


def draw_hidden_in(key, part):
    key = jax.random.fold_in(key, 11)
    key_base, key_rows, key_cols = jax.random.split(key, 3)
    column_pos = jnp.arange(D).astype(jnp.float32) / (D - 1)
    row_scale = jnp.exp(jax.random.uniform(key_rows, (TOKENS, 1), jnp.float32, math.log(0.4), math.log(2.5)))
    base_vals = jax.random.normal(key_base, (TOKENS, D), jnp.float32)
    col_scale = jnp.exp(math.log(3.0) * column_pos + jax.random.uniform(key_cols, (D,), jnp.float32, math.log(0.4), math.log(2.5)))
    return (base_vals * row_scale * col_scale[None, :]).astype(jnp.bfloat16)


def draw_li_rate(key, part):
    key = jax.random.fold_in(key, 23)
    key_pick, key_value = jax.random.split(key, 2)
    slow_share = 0.5
    is_slow = jax.random.uniform(key_pick, (POLES, D), jnp.float32) < slow_share
    uniform_vals = jax.random.uniform(key_value, (POLES, D), jnp.float32)
    slow_low = math.log(0.1 / TOKENS)
    slow_high = math.log(2.0 / TOKENS)
    fast_high = math.log(1.0 / 30.0)
    slow_rate = jnp.exp(slow_low + uniform_vals * (slow_high - slow_low))
    fast_rate = jnp.exp(slow_high + uniform_vals * (fast_high - slow_high))
    return jnp.where(is_slow, slow_rate, fast_rate).astype(jnp.float32)


def shard_levels(own_key, dims, cuts, smallest, high):
    level, own = 1.0, jax.random.fold_in(own_key, 6)
    for axis_at, blocks in cuts:
        heights = jnp.exp(jax.random.uniform(jax.random.fold_in(own, axis_at), (blocks,), jnp.float32, smallest / len(cuts), high / len(cuts)))
        level = level * jnp.repeat(heights, dims[axis_at] // blocks).reshape([-1 if axis == axis_at else 1 for axis in range(len(dims))])
    return level


def gaussian(key, dims, deviation, most, pieces=(), held_as=jnp.bfloat16):
    gain = shard_levels(key, dims, pieces, -0.22, 0.18) if pieces else 1.0
    values = jax.random.normal(key, dims, jnp.float32) * deviation * gain
    return jnp.minimum(jnp.maximum(values, -most), most).astype(held_as)


def setup_inputs(seed: int = 0) -> dict:
    seeds = jax.random.split(jax.random.key(seed), 11)
    hidden_in = draw_hidden_in(jax.random.fold_in(seeds[10], 71), 0)
    query_mr = gaussian(seeds[1], (TOKENS, D), 1.0, 6.0, ((0, 64), (1, 8)))
    key_mr = gaussian(seeds[2], (TOKENS, D), 1.0, 6.0, ((0, 64), (1, 8)))
    value_mr = gaussian(seeds[3], (TOKENS, D), 1.0, 6.0, ((0, 64), (1, 8)))
    query_li = gaussian(seeds[4], (TOKENS, D), 1.0, 6.0, ((0, 64), (1, 8)))
    key_li = gaussian(seeds[5], (TOKENS, D), 1.0, 6.0, ((0, 64), (1, 8)))
    mr_filter = gaussian(seeds[6], (MR_LEN, MR_GROUPS), MR_LEN ** -0.5, 0.5, ((1, 8),))
    li_rate = draw_li_rate(jax.random.fold_in(seeds[10], 71), 0)
    li_residue = gaussian(seeds[8], (POLES, D), 0.25, 4.0, ((1, 8),), jnp.float32)
    norm_gain = jnp.clip(1.0 + 0.15 * jax.random.normal(seeds[9], (D,), jnp.float32), 0.25, 1.75)
    return {"hidden_in": hidden_in, "query_mr": query_mr, "key_mr": key_mr, "value_mr": value_mr, "query_li": query_li, "key_li": key_li, "mr_filter": mr_filter, "li_rate": li_rate, "li_residue": li_residue, "norm_gain": norm_gain}


def toeplitz_band(filter_taps, filter_len):
    group_count = filter_taps.shape[1]
    padded = jnp.concatenate([jnp.zeros((1, group_count), filter_taps.dtype), jnp.flip(filter_taps, 0), jnp.zeros((filter_len, group_count), filter_taps.dtype)], 0)
    repeated = jnp.tile(padded, (filter_len, 1))[:filter_len * 2 * filter_len]
    return repeated.reshape(filter_len, 2 * filter_len, group_count)

def medium_conv(product, mr_filter):
    tokens, channels = product.shape
    filter_len = mr_filter.shape[0]
    group_count = mr_filter.shape[1]
    toeplitz = toeplitz_band(mr_filter.astype(jnp.float32), filter_len)
    padded = jnp.concatenate([jnp.zeros((filter_len, channels), jnp.bfloat16), product], 0)
    blocks = tokens // filter_len
    earlier_rows = padded[:-filter_len].reshape(blocks, filter_len, group_count, channels // group_count)
    latter_rows = padded[filter_len:].reshape(blocks, filter_len, group_count, channels // group_count)

    def one_block(block_index):
        window = jnp.concatenate([earlier_rows[block_index], latter_rows[block_index]], 0).astype(jnp.float32)
        return jnp.einsum('tsg,sgk->tgk', toeplitz, window, precision=lax.Precision.HIGHEST)
    result = lax.map(one_block, jnp.arange(blocks))
    return result.reshape(tokens, channels)

def long_conv(source, li_rate, li_residue):
    block_len = 16
    tokens, channels = source.shape
    pole_count = li_rate.shape[0]
    scaled = li_residue * jnp.sqrt(-jnp.expm1(-2.0 * li_rate))
    lag_steps = jnp.arange(block_len).astype(jnp.float32)
    mode_taps = lax.optimization_barrier(jnp.sum(scaled[None] * jnp.exp(-lag_steps[:, None, None] * li_rate[None]), 1))
    lag_index = jnp.arange(block_len).astype(jnp.int32)
    lag_grid = lag_index[:, None] - lag_index[None, :]
    selector = (lag_grid[:, :, None] == lag_index[None, None, :]).astype(jnp.float32)
    intra_block = jnp.einsum('tsd,dc->tsc', selector, mode_taps, precision=lax.Precision.HIGHEST)
    decay_out = jnp.exp(-(block_len - 1 - lag_steps)[:, None, None] * li_rate[None])
    decay_in = scaled[None] * jnp.exp(-(lag_steps + 1.0)[:, None, None] * li_rate[None])
    block_decay = jnp.exp(-block_len * li_rate)
    blocks_in = source.reshape(tokens // block_len, block_len, channels)

    def advance(state, block_rows):
        local_part = jnp.einsum('tsc,sc->tc', intra_block, block_rows, precision=lax.Precision.HIGHEST)
        from_states = jnp.einsum('tnc,nc->tc', decay_in, state, precision=lax.Precision.HIGHEST)
        new_state = block_decay * state + jnp.einsum('snc,sc->nc', decay_out, block_rows, precision=lax.Precision.HIGHEST)
        return (new_state, local_part + from_states)
    _, outputs = lax.scan(advance, jnp.zeros((pole_count, channels), jnp.float32), blocks_in)
    return outputs.reshape(tokens, channels)

def reference(hidden_in, query_mr, key_mr, value_mr, query_li, key_li, mr_filter, li_rate, li_residue, norm_gain):
    product = (key_mr.astype(jnp.float32) * value_mr.astype(jnp.float32)).astype(jnp.bfloat16)
    conv_mr = medium_conv(product, mr_filter)
    out_mr = (query_mr.astype(jnp.float32) * conv_mr).astype(jnp.bfloat16)
    source = key_li.astype(jnp.float32) * out_mr.astype(jnp.float32)
    conv_li = long_conv(source, li_rate, li_residue)
    combined = hidden_in.astype(jnp.float32) + out_mr.astype(jnp.float32) + query_li.astype(jnp.float32) * conv_li
    inverse_rms = lax.rsqrt(lax.optimization_barrier(jnp.mean(combined * combined, axis=1, keepdims=True)) + 1e-06)
    return (combined * inverse_rms * norm_gain[None, :]).astype(jnp.bfloat16)
```

```python
import jax
import jax.numpy as jnp
from jax import lax
from jax.experimental import pallas as pl
from jax.experimental.pallas import tpu as pltpu
from jax.sharding import Mesh, PartitionSpec as P

F32 = jnp.float32
BF16 = jnp.bfloat16
LANES = 128
SUBS = 8
STEP = 16
SEQ = ("y", "x", "core")
HIGHEST = lax.Precision.HIGHEST
VMEM_LIMIT = 48 * 1024 * 1024


def iota(shape, dim):
    return lax.broadcasted_iota(jnp.int32, shape, dim)


def strided(row):
    return pl.ds(row, SUBS, stride=STEP)


def tile_cols(tile):
    return pl.ds(tile * LANES, LANES)


def spread_row(values, n):
    return jnp.broadcast_to(values[n : n + 1], (SUBS, LANES))


def own_kernel(filter_ref, product_ref, table_ref, bands_ref, conv_ref, taps_ref):
    groups, taps = filter_ref.shape
    channels = product_ref.shape[1]
    width = channels // groups
    per_tile = LANES // width
    row, lane = iota((taps, taps), 0), iota((taps, taps), 1)
    flip = ((row + lane) % taps == 0).astype(BF16)
    flipped = jnp.dot(filter_ref[...], flip, preferred_element_type=F32)
    earlier = lane > row
    lane_group = iota((taps, LANES), 1) // width
    for tile in range(channels // LANES):
        cols = tile_cols(tile)
        latest = product_ref[:, cols]
        conv = jnp.zeros((taps, LANES), F32)
        for part in range(per_tile):
            group = tile * per_tile + part
            one = jnp.broadcast_to(flipped[group : group + 1], (taps, taps))
            circulant = pltpu.roll(one, 0, 1, stride=1, stride_axis=0)
            bands_ref[group] = jnp.where(earlier, circulant, 0.0).astype(BF16)
            band = jnp.where(earlier, 0.0, circulant).astype(BF16)
            result = jnp.dot(band, latest, preferred_element_type=F32)
            conv = jnp.where(lane_group == part, result, conv)
        conv_ref[:, cols] = conv
        decay = jnp.exp(table_ref[1, :, cols] / STEP)
        powers = table_ref[0, :, cols]
        for lag in range(STEP):
            taps_ref[lag : lag + 1, cols] = jnp.sum(powers, 0, keepdims=True)
            powers = powers * decay


def medium_kernel(
    halo_ref, bands_ref, conv_ref, query_ref, key_ref, table_ref,
    out_mr_ref, source_ref, starts_ref, spread_ref,
):
    tokens, channels = halo_ref.shape
    groups = bands_ref.shape[0]
    poles = table_ref.shape[1]
    width = channels // groups
    per_tile = LANES // width
    lane_group = iota((tokens, LANES), 1) // width
    block = iota((SUBS, LANES), 0)
    for tile in range(channels // LANES):
        cols = tile_cols(tile)
        before = halo_ref[:, cols]
        conv = jnp.zeros((tokens, LANES), F32)
        for part in range(per_tile):
            band = bands_ref[tile * per_tile + part]
            result = jnp.dot(band, before, preferred_element_type=F32)
            conv = jnp.where(lane_group == part, result, conv)
        conv = conv + conv_ref[:, cols]
        out_mr = (query_ref[:, cols].astype(F32) * conv).astype(BF16)
        out_mr_ref[:, cols] = out_mr
        source_ref[tile] = key_ref[:, cols].astype(F32) * out_mr.astype(F32)
        gain, fade = table_ref[0, :, cols], table_ref[1, :, cols]
        decay = jnp.exp(fade / STEP)
        jumps = [jnp.exp(fade * k) for k in (1, 2, 4)]
        rows = [source_ref[tile, strided(i), :] for i in range(STEP)]
        last = []
        for n in range(poles):
            one = spread_row(decay, n)
            ends = rows[0]
            for i in range(1, STEP):
                ends = ends * one + rows[i]
            for k, jump in zip((1, 2, 4), jumps):
                shifted = jnp.where(block >= k, pltpu.roll(ends, k, 0), 0.0)
                ends = ends + spread_row(jump, n) * shifted
            shifted = jnp.where(block >= 1, pltpu.roll(ends, 1, 0), 0.0)
            starts_ref[n, :, cols] = shifted * spread_row(gain, n)
            last.append(ends[SUBS - 1 :])
        state = jnp.concatenate(last, 0).astype(BF16)
        half = spread_ref.shape[2]
        for to in range(tile * LANES // half, spread_ref.shape[0], 2):
            spread_ref[to, :, pl.ds(tile * LANES % half, LANES)] = state


def own_half(tile, half):
    start = lax.axis_index("core") * half + tile * LANES
    return pl.ds(pl.multiple_of(start, LANES), LANES)


def scan_stack(stack_ref, cols, step):
    states = [jnp.zeros(step.shape, F32)]
    for j in range(stack_ref.shape[0]):
        states.append(states[-1] * step + stack_ref[j, :, cols].astype(F32))
    return states


def pick(states, position):
    chosen = states[0]
    for j in range(1, len(states)):
        chosen = jnp.where(position == j, states[j], chosen)
    return chosen


def row_kernel(tokens, stack_ref, table_ref, ahead_ref, spread_ref):
    half = stack_ref.shape[2]
    place = lax.axis_index("x")
    for tile in range(half // LANES):
        cols = tile_cols(tile)
        step = jnp.exp(table_ref[1, :, own_half(tile, half)] * (tokens // STEP))
        states = scan_stack(stack_ref, cols, step)
        for core in range(2):
            ahead_ref[core, :, cols] = pick(states[core:-1:2], place)
        state = states[-1].astype(BF16)
        for to in range(spread_ref.shape[0]):
            spread_ref[to, :, cols] = state


def join_kernel(tokens, stack_ref, ahead_ref, table_ref, incoming_ref):
    half = stack_ref.shape[2]
    in_row = lax.axis_size("x") * 2
    first = (lax.axis_index("x") * 2).astype(F32)
    for tile in range(half // LANES):
        cols = tile_cols(tile)
        fade = table_ref[1, :, own_half(tile, half)] * (tokens // STEP)
        states = scan_stack(stack_ref, cols, jnp.exp(fade * in_row))
        above = pick(states[:-1], lax.axis_index("y"))
        for core in range(2):
            reach = jnp.exp(fade * (first + core))
            incoming_ref[core, :, cols] = ahead_ref[core, :, cols] + reach * above


def long_kernel(
    incoming_ref, table_ref, taps_ref, source_ref, starts_ref,
    hidden_ref, out_mr_ref, query_ref, norm_ref,
    scaled_ref, squares_ref, conv_ref,
):
    tokens, channels = hidden_ref.shape
    poles = table_ref.shape[1]
    half = incoming_ref.shape[3]
    core = lax.axis_index("core")
    block = iota((SUBS, LANES), 0).astype(F32)
    squares = jnp.zeros((tokens, LANES), F32)
    for tile in range(channels // LANES):
        cols = tile_cols(tile)
        gain, fade = table_ref[0, :, cols], table_ref[1, :, cols]
        decay = jnp.exp(fade / STEP)
        place = tile * LANES
        incoming = incoming_ref[place // half, core, :, pl.ds(place % half, LANES)] * gain
        rows = [source_ref[tile, strided(i), :] for i in range(STEP)]
        sums = [jnp.zeros((SUBS, LANES), F32)] * STEP
        for lag in range(STEP):
            tap = jnp.broadcast_to(taps_ref[lag : lag + 1, cols], (SUBS, LANES))
            for i in range(lag, STEP):
                sums[i] = sums[i] + tap * rows[i - lag]
        for n in range(poles):
            one = spread_row(decay, n)
            entering = jnp.exp(block * spread_row(fade, n)) * spread_row(incoming, n)
            mode = starts_ref[n, :, cols] + entering
            for i in range(STEP):
                mode = mode * one
                sums[i] = sums[i] + mode
        for i in range(STEP):
            conv_ref[strided(i), :] = sums[i]
        combined = (
            hidden_ref[:, cols].astype(F32)
            + out_mr_ref[:, cols].astype(F32)
            + query_ref[:, cols].astype(F32) * conv_ref[...]
        )
        scaled_ref[:, cols] = combined * norm_ref[:, cols]
        squares = squares + combined * combined
    total = jnp.sum(squares.T, 0, keepdims=True)
    squares_ref[...] = jnp.broadcast_to(total, squares_ref.shape)


def call(kernel, outs, scratch=(), cost=None):
    return pl.pallas_call(
        kernel,
        out_shape=[jax.ShapeDtypeStruct(shape, dtype) for shape, dtype in outs],
        scratch_shapes=[pltpu.VMEM(shape, dtype) for shape, dtype in scratch],
        compiler_params=pltpu.CompilerParams(vmem_limit_bytes=VMEM_LIMIT),
        cost_estimate=cost,
    )


def per_device(
    hidden_in,
    query_mr,
    key_mr,
    value_mr,
    query_li,
    key_li,
    mr_filter,
    li_rate,
    li_residue,
    norm_gain,
):
    tokens, channels = key_mr.shape
    filter_len, groups = mr_filter.shape
    poles = li_rate.shape[0]
    tiles = channels // LANES
    half = channels // 2
    ys = lax.axis_size("y")
    in_row = lax.axis_size("x") * lax.axis_size("core")
    product = (key_mr.astype(F32) * value_mr.astype(F32)).astype(BF16)
    halo = lax.ppermute(product, SEQ, [(i, i + 1) for i in range(ys * in_row - 1)])
    gain = li_residue * jnp.sqrt(-jnp.expm1(-2.0 * li_rate))
    table = jnp.stack([gain, li_rate * -float(STEP)])
    cost = pl.CostEstimate(
        flops=2 * groups * filter_len * filter_len * LANES, bytes_accessed=2**22, transcendentals=0
    )
    bands, own, taps = call(
        own_kernel,
        [
            ((groups, filter_len, filter_len), BF16),
            ((tokens, channels), F32),
            ((STEP, channels), F32),
        ],
        cost=cost,
    )(mr_filter.T, product, table)
    out_mr, source, starts, states = call(
        medium_kernel,
        [
            ((tokens, channels), BF16),
            ((tiles, tokens, LANES), F32),
            ((poles, SUBS, channels), F32),
            ((in_row, poles, half), BF16),
        ],
    )(halo, bands, own, query_mr, key_li, table)
    states = lax.all_to_all(states, ("x", "core"), 0, 0, tiled=True)
    ahead, rows = call(
        lambda *refs: row_kernel(tokens, *refs),
        [((2, poles, half), F32), ((ys, poles, half), BF16)],
    )(states, table)
    rows = lax.all_to_all(rows, "y", 0, 0, tiled=True)
    (incoming,) = call(lambda *refs: join_kernel(tokens, *refs), [((2, poles, half), F32)])(
        rows, ahead, table
    )
    incoming = lax.all_gather(incoming, "core")
    scaled, squares = call(
        long_kernel,
        [((tokens, channels), F32), ((SUBS, tokens), F32)],
        [((tokens, LANES), F32)],
    )(
        incoming, table, taps, source, starts,
        hidden_in, out_mr, query_li, norm_gain.reshape(1, channels),
    )
    chans = lax.axis_size("chan")
    squares = lax.all_to_all(squares.reshape(chans, 1, tokens), "chan", 0, 0, tiled=True)
    inverse_rms = lax.rsqrt(jnp.sum(squares, (0, 1)) / (channels * chans) + 1e-06)
    return (scaled * inverse_rms[:, None]).astype(BF16)


def solution(mesh):
    seq, chan = mesh.devices.shape
    xs = 4 if seq >= 64 else 2
    fine = Mesh(mesh.devices.reshape(seq // (2 * xs), xs, 2, chan), ("y", "x", "core", "chan"))
    both = P(SEQ, "chan")
    last = P(None, "chan")
    return jax.shard_map(
        per_device,
        mesh=fine,
        in_specs=(both,) * 6 + (last,) * 3 + (P("chan"),),
        out_specs=both,
        check_vma=False,
    )
```

```python
import jax
import jax.numpy as jnp
from jax import lax
from jax.experimental import pallas as pl
from jax.experimental.pallas import tpu as pltpu
from jax.sharding import Mesh, PartitionSpec as P

F32 = jnp.float32
BF16 = jnp.bfloat16
LANES = 128
SUBS = 8
STEP = 16
JUMPS = (1, 2, 4)
MODES = 8
SEQ = ("y", "x", "core")
VMEM_LIMIT = 20 * 1024 * 1024


def iota(shape, dim):
    return lax.broadcasted_iota(jnp.int32, shape, dim)


def strided(row):
    return pl.ds(row, SUBS, stride=STEP)


def tile_cols(tile):
    return pl.ds(tile * LANES, LANES)


def spread_row(values, n):
    return jnp.broadcast_to(values[n : n + 1], (SUBS, LANES))


def group_rows(values, width):
    rows, lanes = values.shape
    member = iota((2 * SUBS, lanes), 1) // width
    parts = []
    for part in range(lanes // width):
        mask = (member == part).astype(F32).astype(BF16)
        parts.append(values * jnp.concatenate([mask] * (rows // (2 * SUBS)), 0))
    return jnp.concatenate(parts, 0)


def lost_share(rate):
    square = rate * rate
    series = 1.0 + square / 110.0
    for factor in (72.0, 42.0, 20.0, 6.0):
        series = 1.0 + square / factor * series
    small = 2.0 * jnp.exp(-rate) * rate * series
    return jnp.where(rate < 0.5, small, 1.0 - jnp.exp(-2.0 * rate))


def locate(tile, refs):
    for ref in refs:
        if tile < ref.shape[-1] // LANES:
            return ref, tile
        tile -= ref.shape[-1] // LANES


def part_kernel(first, product_ref, *refs):
    refs[-1][...] = product_ref[:, first : first + refs[-1].shape[1]]


def own_kernel(
    filter_ref, rate_ref, residue_ref, product_0, product_1,
    bands_ref, conv_ref, taps_ref, fade_ref, weights_ref,
):
    groups, taps = filter_ref.shape
    channels = rate_ref.shape[1]
    width = channels // groups
    per_tile = LANES // width
    row, lane = iota((taps, taps), 0), iota((taps, taps), 1)
    flip = ((row + lane) % taps == 0).astype(BF16)
    flipped = jnp.dot(filter_ref[...], flip, preferred_element_type=F32)
    earlier = lane > row
    block = iota((SUBS, LANES), 0)
    for tile in range(channels // LANES):
        cols = tile_cols(tile)
        bands = []
        for part in range(per_tile):
            group = tile * per_tile + part
            one = jnp.broadcast_to(flipped[group : group + 1], (taps, taps))
            circulant = pltpu.roll(one, 0, 1, stride=1, stride_axis=0)
            bands_ref[tile, :, tile_cols(part)] = jnp.where(earlier, circulant, 0.0).astype(BF16)
            bands.append(jnp.where(earlier, 0.0, circulant).astype(BF16))
        product_ref, place = locate(tile, (product_0, product_1))
        product = product_ref[:, tile_cols(place)]
        conv_ref[:, cols] = jnp.dot(
            jnp.concatenate(bands, 1), group_rows(product, width), preferred_element_type=F32
        )
        rate = rate_ref[:, cols]
        gain = residue_ref[:, cols] * jnp.sqrt(lost_share(rate))
        fade = rate * -float(STEP)
        fade_ref[:, cols] = fade
        decay = jnp.exp(fade / STEP)
        powers = gain
        for lag in range(STEP):
            taps_ref[lag : lag + 1, cols] = jnp.sum(powers, 0, keepdims=True)
            powers = powers * decay
        jumps = [jnp.exp(fade * k) for k in JUMPS]
        start = gain * decay
        for n in range(gain.shape[0]):
            weights_ref[0, n, :, cols] = spread_row(decay, n)
            for k, jump in zip(JUMPS, jumps):
                place = JUMPS.index(k) + 1
                weights_ref[place, n, :, cols] = jnp.where(block >= k, spread_row(jump, n), 0.0)
            begin = spread_row(start, n)
            weights_ref[4, n, :, cols] = jnp.where(block >= 1, begin, 0.0)
            reach = jnp.exp(block.astype(F32) * spread_row(fade, n))
            weights_ref[5, n, :, cols] = begin * reach


def medium_kernel(
    start, halo_ref, bands_ref, conv_ref, query_ref, key_ref, weights_ref, *refs
):
    *others, out_mr_ref, source_ref, starts_ref, state_ref = refs
    poles = weights_ref.shape[1]
    width = LANES * LANES // bands_ref.shape[2]
    states = [other[:, tile_cols(i)] for other in others for i in range(other.shape[1] // LANES)]
    for tile in range(halo_ref.shape[1] // LANES):
        whole = start + tile
        cols, here = tile_cols(whole), tile_cols(tile)
        conv = conv_ref[:, cols] + jnp.dot(
            bands_ref[whole], group_rows(halo_ref[:, here], width), preferred_element_type=F32
        )
        out_mr = (query_ref[:, cols].astype(F32) * conv).astype(BF16)
        out_mr_ref[:, here] = out_mr
        source_ref[tile] = key_ref[:, cols].astype(F32) * out_mr.astype(F32)
        rows = [source_ref[tile, strided(i), :] for i in range(STEP)]
        last = []
        for first in range(0, poles, MODES):
            modes = range(first, min(first + MODES, poles))
            decays = [weights_ref[0, n, :, cols] for n in modes]
            ends = [rows[0]] * len(modes)
            for i in range(1, STEP):
                ends = [end * decay + rows[i] for end, decay in zip(ends, decays)]
            for place, k in enumerate(JUMPS):
                weights = [weights_ref[place + 1, n, :, cols] for n in modes]
                ends = [end + w * pltpu.roll(end, k, 0) for end, w in zip(ends, weights)]
            for n, end in zip(modes, ends):
                starts_ref[n, :, here] = weights_ref[4, n, :, cols] * pltpu.roll(end, 1, 0)
                last.append(end[SUBS - 1 :])
        states.append(jnp.concatenate(last, 0).astype(BF16))
    if not others:
        for tile, state in enumerate(states):
            state_ref[:, tile_cols(tile)] = state
        return
    half = state_ref.shape[2] // LANES
    for tile, state in enumerate(states):
        for to in range(tile // half, state_ref.shape[0], 2):
            state_ref[to, :, tile_cols(tile % half)] = state


def own_half(tile, half):
    start = lax.axis_index("core") * half + tile * LANES
    return pl.ds(pl.multiple_of(start, LANES), LANES)


def tree_sum(values):
    while len(values) > 1:
        values = [a + b for a, b in zip(values[::2], values[1::2])] + values[len(values) // 2 * 2 :]
    return values[0]


def scan_stack(stack_ref, cols, step):
    states = [jnp.zeros(step.shape, F32)]
    for j in range(stack_ref.shape[0]):
        states.append(states[-1] * step + stack_ref[j, :, cols].astype(F32))
    return states


def pick(states, position):
    chosen = states[0]
    for j in range(1, len(states)):
        chosen = jnp.where(position == j, states[j], chosen)
    return chosen


def row_kernel(tokens, stack_ref, fade_ref, ahead_ref, spread_ref):
    half = stack_ref.shape[2]
    for tile in range(half // LANES):
        cols = tile_cols(tile)
        step = jnp.exp(fade_ref[:, own_half(tile, half)] * (tokens // STEP))
        states = scan_stack(stack_ref, cols, step)
        for core in range(2):
            ahead_ref[core, :, cols] = pick(states[core:-1:2], lax.axis_index("x"))
        state = states[-1].astype(BF16)
        for to in range(spread_ref.shape[0]):
            spread_ref[to, :, cols] = state


def join_kernel(tokens, stack_ref, ahead_ref, fade_ref, incoming_ref):
    half = stack_ref.shape[2]
    in_row = lax.axis_size("x") * 2
    first = (lax.axis_index("x") * 2).astype(F32)
    for tile in range(half // LANES):
        cols = tile_cols(tile)
        fade = fade_ref[:, own_half(tile, half)] * (tokens // STEP)
        states = scan_stack(stack_ref, cols, jnp.exp(fade * in_row))
        above = pick(states[:-1], lax.axis_index("y"))
        for core in range(2):
            reach = jnp.exp(fade * (first + core))
            incoming_ref[core, :, cols] = ahead_ref[core, :, cols] + reach * above


def long_kernel(
    incoming_ref, taps_ref, weights_ref, hidden_ref, query_ref, norm_ref,
    out_mr_0, source_0, starts_0, out_mr_1, source_1, starts_1,
    scaled_ref, squares_ref, conv_ref,
):
    tokens, channels = hidden_ref.shape
    poles, half = incoming_ref.shape[2:]
    core = lax.axis_index("core")
    squares = jnp.zeros((tokens, LANES), F32)
    for tile in range(channels // LANES):
        cols = tile_cols(tile)
        out_mr_ref, place = locate(tile, (out_mr_0, out_mr_1))
        source_ref, starts_ref = (source_0, starts_0) if out_mr_ref is out_mr_0 else (source_1, starts_1)
        here = tile_cols(place)
        side = tile * LANES // half
        incoming = incoming_ref[side, core, :, tile_cols(tile % (half // LANES))]
        rows = [source_ref[place, strided(i), :] for i in range(STEP)]
        sums = [jnp.zeros((SUBS, LANES), F32)] * STEP
        for lag in range(STEP):
            tap = jnp.broadcast_to(taps_ref[lag : lag + 1, cols], (SUBS, LANES))
            for i in range(lag, STEP):
                sums[i] = sums[i] + tap * rows[i - lag]
        for first in range(0, poles, MODES):
            modes = range(first, min(first + MODES, poles))
            decays = [weights_ref[0, n, :, cols] for n in modes]
            values = [
                starts_ref[n, :, here] + weights_ref[5, n, :, cols] * spread_row(incoming, n)
                for n in modes
            ]
            for i in range(STEP):
                if i:
                    values = [value * decay for value, decay in zip(values, decays)]
                sums[i] = sums[i] + tree_sum(values)
        for i in range(STEP):
            conv_ref[strided(i), :] = sums[i]
        combined = (
            hidden_ref[:, cols].astype(F32)
            + out_mr_ref[:, here].astype(F32)
            + query_ref[:, cols].astype(F32) * conv_ref[...]
        )
        scaled_ref[:, cols] = combined * norm_ref[:, cols]
        squares = squares + combined * combined
    total = jnp.sum(squares.T, 0, keepdims=True)
    squares_ref[...] = jnp.broadcast_to(total, squares_ref.shape)


def norm_kernel(total, scaled_ref, squares_ref, out_ref):
    tokens, channels = scaled_ref.shape
    square = jnp.sum(squares_ref[...], 0, keepdims=True)
    inverse = jnp.broadcast_to(lax.rsqrt(square / total + 1e-06), (tokens, tokens)).T
    for tile in range(channels // LANES):
        cols = tile_cols(tile)
        out_ref[:, cols] = (scaled_ref[:, cols] * inverse).astype(BF16)


def call(kernel, outs, scratch=(), cost=None):
    return pl.pallas_call(
        kernel,
        out_shape=[jax.ShapeDtypeStruct(shape, dtype) for shape, dtype in outs],
        scratch_shapes=[pltpu.VMEM(shape, dtype) for shape, dtype in scratch],
        compiler_params=pltpu.CompilerParams(vmem_limit_bytes=VMEM_LIMIT),
        cost_estimate=cost,
    )


def per_device(
    hidden_in,
    query_mr,
    key_mr,
    value_mr,
    query_li,
    key_li,
    mr_filter,
    li_rate,
    li_residue,
    norm_gain,
):
    tokens, channels = key_mr.shape
    filter_len, groups = mr_filter.shape
    poles = li_rate.shape[0]
    tiles = channels // LANES
    half = channels // 2
    ys = lax.axis_size("y")
    in_row = lax.axis_size("x") * lax.axis_size("core")
    long_op = pl.CostEstimate(
        flops=16 * groups * filter_len * filter_len * LANES, bytes_accessed=2**22, transcendentals=0
    )
    product = (key_mr.astype(F32) * value_mr.astype(F32)).astype(BF16)
    route = [(i, i + 1) for i in range(ys * in_row - 1)]
    cut = tiles * 5 // 8
    sizes = ((0, cut), (cut, tiles - cut))
    parts = []
    for first, size in sizes:
        parts += call(
            lambda *refs, first=first: part_kernel(first * LANES, *refs),
            [((tokens, size * LANES), BF16)],
            cost=long_op,
        )(product, *parts)
    halos = [lax.ppermute(part, SEQ, route) for part in parts]
    bands, own, taps, fade, weights = call(
        own_kernel,
        [
            ((tiles, filter_len, LANES * groups * LANES // channels), BF16),
            ((tokens, channels), F32),
            ((STEP, channels), F32),
            ((poles, channels), F32),
            ((6, poles, SUBS, channels), F32),
        ],
        cost=long_op,
    )(mr_filter.T, li_rate, li_residue, *parts)
    done, states = [], []
    for (first, size), halo in zip(sizes, halos):
        last = first + size == tiles
        *mixed, state = call(
            lambda *refs, first=first: medium_kernel(first, *refs),
            [
                ((tokens, size * LANES), BF16),
                ((size, tokens, LANES), F32),
                ((poles, SUBS, size * LANES), F32),
                ((in_row, poles, half) if last else (poles, size * LANES), BF16),
            ],
        )(halo, bands, own, query_mr, key_li, weights, *states)
        done += mixed
        states = [state]
    (states,) = states
    states = lax.all_to_all(states, ("x", "core"), 0, 0, tiled=True)
    ahead, rows = call(
        lambda *refs: row_kernel(tokens, *refs),
        [((2, poles, half), F32), ((ys, poles, half), BF16)],
    )(states, fade)
    rows = lax.all_to_all(rows, "y", 0, 0, tiled=True)
    (incoming,) = call(lambda *refs: join_kernel(tokens, *refs), [((2, poles, half), F32)])(
        rows, ahead, fade
    )
    incoming = lax.all_gather(incoming, "core")
    scaled, squares = call(
        long_kernel,
        [((tokens, channels), F32), ((SUBS, tokens), F32)],
        [((tokens, LANES), F32)],
    )(
        incoming, taps, weights, hidden_in, query_li, norm_gain.reshape(1, channels), *done
    )
    chans = lax.axis_size("chan")
    squares = lax.all_to_all(squares.reshape(chans, 1, tokens), "chan", 0, 0, tiled=True)
    (out,) = call(
        lambda *refs: norm_kernel(channels * chans, *refs), [((tokens, channels), BF16)]
    )(scaled, squares.reshape(chans, tokens))
    return out


def solution(mesh):
    seq, chan = mesh.devices.shape
    xs = 4 if seq >= 64 else 2
    fine = Mesh(mesh.devices.reshape(seq // (2 * xs), xs, 2, chan), ("y", "x", "core", "chan"))
    both = P(SEQ, "chan")
    last = P(None, "chan")
    return jax.shard_map(
        per_device,
        mesh=fine,
        in_specs=(both,) * 6 + (last,) * 3 + (P("chan"),),
        out_specs=both,
        check_vma=False,
    )
```

```python
import jax
import jax.numpy as jnp
from jax import lax
from jax.experimental import pallas as pl
from jax.experimental.pallas import tpu as pltpu
from jax.sharding import Mesh, PartitionSpec as P

F32 = jnp.float32
BF16 = jnp.bfloat16
LANES = 128
SUBS = 8
STEP = 16
JUMPS = (1, 2, 4)
MODES = 8
SEQ = ("y", "x", "core")
VMEM_LIMIT = 20 * 1024 * 1024


def iota(shape, dim):
    return lax.broadcasted_iota(jnp.int32, shape, dim)


def strided(row):
    return pl.ds(row, SUBS, stride=STEP)


def tile_cols(tile):
    return pl.ds(tile * LANES, LANES)


def spread_row(values, n):
    return jnp.broadcast_to(values[n : n + 1], (SUBS, LANES))


def group_rows(values, width):
    rows, lanes = values.shape
    member = iota((2 * SUBS, lanes), 1) // width
    parts = []
    for part in range(lanes // width):
        mask = (member == part).astype(F32).astype(BF16)
        parts.append(values * jnp.concatenate([mask] * (rows // (2 * SUBS)), 0))
    return jnp.concatenate(parts, 0)


def lost_share(rate):
    square = rate * rate
    series = 1.0 + square / 110.0
    for factor in (72.0, 42.0, 20.0, 6.0):
        series = 1.0 + square / factor * series
    small = 2.0 * jnp.exp(-rate) * rate * series
    return jnp.where(rate < 0.5, small, 1.0 - jnp.exp(-2.0 * rate))


def locate(tile, refs):
    for ref in refs:
        if tile < ref.shape[-1] // LANES:
            return ref, tile
        tile -= ref.shape[-1] // LANES


def part_kernel(first, product_ref, *refs):
    refs[-1][...] = product_ref[:, first : first + refs[-1].shape[1]]


def own_kernel(
    filter_ref, rate_ref, residue_ref, product_0, product_1,
    bands_ref, lower_ref, conv_ref, taps_ref, fade_ref, weights_ref,
):
    groups, taps = filter_ref.shape
    channels = rate_ref.shape[1]
    width = channels // groups
    per_tile = LANES // width
    row, lane = iota((taps, taps), 0), iota((taps, taps), 1)
    flip = ((row + lane) % taps == 0).astype(BF16)
    flipped = jnp.dot(filter_ref[...], flip, preferred_element_type=F32)
    earlier = lane > row
    middle = taps // 2
    block = iota((SUBS, LANES), 0)
    for tile in range(channels // LANES):
        cols = tile_cols(tile)
        bands = []
        for part in range(per_tile):
            group = tile * per_tile + part
            one = jnp.broadcast_to(flipped[group : group + 1], (taps, taps))
            circulant = pltpu.roll(one, 0, 1, stride=1, stride_axis=0)
            band = jnp.where(earlier, circulant, 0.0)
            bands_ref[tile, :, tile_cols(part)] = band[:middle].astype(BF16)
            if part % 2 == 0:
                turned = pltpu.roll(one, middle, 1, stride=1, stride_axis=0)[middle:]
                left = jnp.where(lane[:middle] > row[:middle], turned, 0.0)
            else:
                pair = jnp.where(lane[:middle] < middle, left, band[middle:])
                lower_ref[tile, :, tile_cols(part // 2)] = pair.astype(BF16)
            bands.append(jnp.where(earlier, 0.0, circulant).astype(BF16))
        product_ref, place = locate(tile, (product_0, product_1))
        product = product_ref[:, tile_cols(place)]
        conv_ref[:, cols] = jnp.dot(
            jnp.concatenate(bands, 1), group_rows(product, width), preferred_element_type=F32
        )
        rate = rate_ref[:, cols]
        gain = residue_ref[:, cols] * jnp.sqrt(lost_share(rate))
        fade = rate * -float(STEP)
        fade_ref[:, cols] = fade
        decay = jnp.exp(fade / STEP)
        powers = gain
        for lag in range(STEP):
            taps_ref[lag : lag + 1, cols] = jnp.sum(powers, 0, keepdims=True)
            powers = powers * decay
        jumps = [jnp.exp(fade * k) for k in JUMPS]
        start = gain * decay
        for n in range(gain.shape[0]):
            weights_ref[0, n, :, cols] = spread_row(decay, n)
            for k, jump in zip(JUMPS, jumps):
                place = JUMPS.index(k) + 1
                weights_ref[place, n, :, cols] = jnp.where(block >= k, spread_row(jump, n), 0.0)
            begin = spread_row(start, n)
            weights_ref[4, n, :, cols] = jnp.where(block >= 1, begin, 0.0)
            reach = jnp.exp(block.astype(F32) * spread_row(fade, n))
            weights_ref[5, n, :, cols] = begin * reach


def medium_kernel(
    start, halo_ref, bands_ref, lower_ref, conv_ref, query_ref, key_ref, weights_ref, *refs
):
    *others, out_mr_ref, source_ref, starts_ref, state_ref = refs
    poles = weights_ref.shape[1]
    width = LANES * LANES // bands_ref.shape[2]
    states = [other[:, tile_cols(i)] for other in others for i in range(other.shape[1] // LANES)]
    for tile in range(halo_ref.shape[1] // LANES):
        whole = start + tile
        cols, here = tile_cols(whole), tile_cols(tile)
        upper = jnp.dot(
            bands_ref[whole], group_rows(halo_ref[:, here], width), preferred_element_type=F32
        )
        later = halo_ref[bands_ref.shape[1] :, here]
        lower = jnp.dot(lower_ref[whole], group_rows(later, width), preferred_element_type=F32)
        conv = conv_ref[:, cols] + jnp.concatenate([upper, lower], 0)
        out_mr = (query_ref[:, cols].astype(F32) * conv).astype(BF16)
        out_mr_ref[:, here] = out_mr
        source_ref[tile] = key_ref[:, cols].astype(F32) * out_mr.astype(F32)
        rows = [source_ref[tile, strided(i), :] for i in range(STEP)]
        last = []
        for first in range(0, poles, MODES):
            modes = range(first, min(first + MODES, poles))
            decays = [weights_ref[0, n, :, cols] for n in modes]
            ends = [rows[0]] * len(modes)
            for i in range(1, STEP):
                ends = [end * decay + rows[i] for end, decay in zip(ends, decays)]
            for place, k in enumerate(JUMPS):
                weights = [weights_ref[place + 1, n, :, cols] for n in modes]
                ends = [end + w * pltpu.roll(end, k, 0) for end, w in zip(ends, weights)]
            for n, end in zip(modes, ends):
                starts_ref[n, :, here] = weights_ref[4, n, :, cols] * pltpu.roll(end, 1, 0)
                last.append(end[SUBS - 1 :])
        states.append(jnp.concatenate(last, 0).astype(BF16))
    if not others:
        for tile, state in enumerate(states):
            state_ref[:, tile_cols(tile)] = state
        return
    half = state_ref.shape[2] // LANES
    for tile, state in enumerate(states):
        for to in range(tile // half, state_ref.shape[0], 2):
            state_ref[to, :, tile_cols(tile % half)] = state


def own_half(tile, half):
    start = lax.axis_index("core") * half + tile * LANES
    return pl.ds(pl.multiple_of(start, LANES), LANES)


def tree_sum(values):
    while len(values) > 1:
        values = [a + b for a, b in zip(values[::2], values[1::2])] + values[len(values) // 2 * 2 :]
    return values[0]


def scan_stack(stack_ref, cols, step):
    states = [jnp.zeros(step.shape, F32)]
    for j in range(stack_ref.shape[0]):
        states.append(states[-1] * step + stack_ref[j, :, cols].astype(F32))
    return states


def pick(states, position):
    chosen = states[0]
    for j in range(1, len(states)):
        chosen = jnp.where(position == j, states[j], chosen)
    return chosen


def row_kernel(tokens, stack_ref, fade_ref, ahead_ref, spread_ref):
    half = stack_ref.shape[2]
    for tile in range(half // LANES):
        cols = tile_cols(tile)
        step = jnp.exp(fade_ref[:, own_half(tile, half)] * (tokens // STEP))
        states = scan_stack(stack_ref, cols, step)
        for core in range(2):
            ahead_ref[core, :, cols] = pick(states[core:-1:2], lax.axis_index("x"))
        state = states[-1].astype(BF16)
        for to in range(spread_ref.shape[0]):
            spread_ref[to, :, cols] = state


def join_kernel(tokens, stack_ref, ahead_ref, fade_ref, incoming_ref):
    half = stack_ref.shape[2]
    in_row = lax.axis_size("x") * 2
    first = (lax.axis_index("x") * 2).astype(F32)
    for tile in range(half // LANES):
        cols = tile_cols(tile)
        fade = fade_ref[:, own_half(tile, half)] * (tokens // STEP)
        states = scan_stack(stack_ref, cols, jnp.exp(fade * in_row))
        above = pick(states[:-1], lax.axis_index("y"))
        for core in range(2):
            reach = jnp.exp(fade * (first + core))
            incoming_ref[core, :, cols] = ahead_ref[core, :, cols] + reach * above


def long_kernel(
    incoming_ref, taps_ref, weights_ref, hidden_ref, query_ref, norm_ref,
    out_mr_0, source_0, starts_0, out_mr_1, source_1, starts_1,
    scaled_ref, squares_ref, conv_ref,
):
    tokens, channels = hidden_ref.shape
    poles, half = incoming_ref.shape[2:]
    core = lax.axis_index("core")
    squares = jnp.zeros((tokens, LANES), F32)
    for tile in range(channels // LANES):
        cols = tile_cols(tile)
        out_mr_ref, place = locate(tile, (out_mr_0, out_mr_1))
        source_ref, starts_ref = (source_0, starts_0) if out_mr_ref is out_mr_0 else (source_1, starts_1)
        here = tile_cols(place)
        side = tile * LANES // half
        incoming = incoming_ref[side, core, :, tile_cols(tile % (half // LANES))]
        rows = [source_ref[place, strided(i), :] for i in range(STEP)]
        sums = [jnp.zeros((SUBS, LANES), F32)] * STEP
        for lag in range(STEP):
            tap = jnp.broadcast_to(taps_ref[lag : lag + 1, cols], (SUBS, LANES))
            for i in range(lag, STEP):
                sums[i] = sums[i] + tap * rows[i - lag]
        for first in range(0, poles, MODES):
            modes = range(first, min(first + MODES, poles))
            decays = [weights_ref[0, n, :, cols] for n in modes]
            values = [
                starts_ref[n, :, here] + weights_ref[5, n, :, cols] * spread_row(incoming, n)
                for n in modes
            ]
            for i in range(STEP):
                if i:
                    values = [value * decay for value, decay in zip(values, decays)]
                sums[i] = sums[i] + tree_sum(values)
        for i in range(STEP):
            conv_ref[strided(i), :] = sums[i]
        combined = (
            hidden_ref[:, cols].astype(F32)
            + out_mr_ref[:, here].astype(F32)
            + query_ref[:, cols].astype(F32) * conv_ref[...]
        )
        scaled_ref[:, cols] = combined * norm_ref[:, cols]
        squares = squares + combined * combined
    total = jnp.sum(squares.T, 0, keepdims=True)
    squares_ref[...] = jnp.broadcast_to(total, squares_ref.shape)


def norm_kernel(total, scaled_ref, squares_ref, out_ref):
    tokens, channels = scaled_ref.shape
    square = jnp.sum(squares_ref[...], 0, keepdims=True)
    inverse = jnp.broadcast_to(lax.rsqrt(square / total + 1e-06), (tokens, tokens)).T
    for tile in range(channels // LANES):
        cols = tile_cols(tile)
        out_ref[:, cols] = (scaled_ref[:, cols] * inverse).astype(BF16)


def call(kernel, outs, scratch=(), cost=None):
    return pl.pallas_call(
        kernel,
        out_shape=[jax.ShapeDtypeStruct(shape, dtype) for shape, dtype in outs],
        scratch_shapes=[pltpu.VMEM(shape, dtype) for shape, dtype in scratch],
        compiler_params=pltpu.CompilerParams(vmem_limit_bytes=VMEM_LIMIT),
        cost_estimate=cost,
    )


def per_device(
    hidden_in,
    query_mr,
    key_mr,
    value_mr,
    query_li,
    key_li,
    mr_filter,
    li_rate,
    li_residue,
    norm_gain,
):
    tokens, channels = key_mr.shape
    filter_len, groups = mr_filter.shape
    poles = li_rate.shape[0]
    tiles = channels // LANES
    half = channels // 2
    ys = lax.axis_size("y")
    in_row = lax.axis_size("x") * lax.axis_size("core")
    long_op = pl.CostEstimate(
        flops=16 * groups * filter_len * filter_len * LANES, bytes_accessed=2**22, transcendentals=0
    )
    product = (key_mr.astype(F32) * value_mr.astype(F32)).astype(BF16)
    route = [(i, i + 1) for i in range(ys * in_row - 1)]
    cut = tiles * 5 // 8
    sizes = ((0, cut), (cut, tiles - cut))
    parts = []
    for first, size in sizes:
        parts += call(
            lambda *refs, first=first: part_kernel(first * LANES, *refs),
            [((tokens, size * LANES), BF16)],
            cost=long_op,
        )(product, *parts)
    halos = [lax.ppermute(part, SEQ, route) for part in parts]
    bands, lower, own, taps, fade, weights = call(
        own_kernel,
        [
            ((tiles, filter_len // 2, filter_len * groups // tiles), BF16),
            ((tiles, filter_len // 2, filter_len // 2 * groups // tiles), BF16),
            ((tokens, channels), F32),
            ((STEP, channels), F32),
            ((poles, channels), F32),
            ((6, poles, SUBS, channels), F32),
        ],
        cost=long_op,
    )(mr_filter.T, li_rate, li_residue, *parts)
    done, states = [], []
    for (first, size), halo in zip(sizes, halos):
        last = first + size == tiles
        *mixed, state = call(
            lambda *refs, first=first: medium_kernel(first, *refs),
            [
                ((tokens, size * LANES), BF16),
                ((size, tokens, LANES), F32),
                ((poles, SUBS, size * LANES), F32),
                ((in_row, poles, half) if last else (poles, size * LANES), BF16),
            ],
        )(halo, bands, lower, own, query_mr, key_li, weights, *states)
        done += mixed
        states = [state]
    (states,) = states
    states = lax.all_to_all(states, ("x", "core"), 0, 0, tiled=True)
    ahead, rows = call(
        lambda *refs: row_kernel(tokens, *refs),
        [((2, poles, half), F32), ((ys, poles, half), BF16)],
    )(states, fade)
    rows = lax.all_to_all(rows, "y", 0, 0, tiled=True)
    (incoming,) = call(lambda *refs: join_kernel(tokens, *refs), [((2, poles, half), F32)])(
        rows, ahead, fade
    )
    incoming = lax.all_gather(incoming, "core")
    scaled, squares = call(
        long_kernel,
        [((tokens, channels), F32), ((SUBS, tokens), F32)],
        [((tokens, LANES), F32)],
    )(
        incoming, taps, weights, hidden_in, query_li, norm_gain.reshape(1, channels), *done
    )
    chans = lax.axis_size("chan")
    squares = lax.all_to_all(squares.reshape(chans, 1, tokens), "chan", 0, 0, tiled=True)
    (out,) = call(
        lambda *refs: norm_kernel(channels * chans, *refs), [((tokens, channels), BF16)]
    )(scaled, squares.reshape(chans, tokens))
    return out


def solution(mesh):
    seq, chan = mesh.devices.shape
    xs = 4 if seq >= 64 else 2
    fine = Mesh(mesh.devices.reshape(seq // (2 * xs), xs, 2, chan), ("y", "x", "core", "chan"))
    both = P(SEQ, "chan")
    last = P(None, "chan")
    return jax.shard_map(
        per_device,
        mesh=fine,
        in_specs=(both,) * 6 + (last,) * 3 + (P("chan"),),
        out_specs=both,
        check_vma=False,
    )
```

```python
import jax
import jax.numpy as jnp
from jax import lax
from jax.experimental import pallas as pl
from jax.experimental.pallas import tpu as pltpu
from jax.sharding import Mesh, PartitionSpec as P

F32 = jnp.float32
BF16 = jnp.bfloat16
LANES = 128
SUBS = 8
STEP = 16
JUMPS = (1, 2, 4)
MODES = 8
SEQ = ("y", "x", "core")
VMEM_LIMIT = 20 * 1024 * 1024


def iota(shape, dim):
    return lax.broadcasted_iota(jnp.int32, shape, dim)


def strided(row):
    return pl.ds(row, SUBS, stride=STEP)


def tile_cols(tile):
    return pl.ds(tile * LANES, LANES)


def spread_row(values, n):
    return jnp.broadcast_to(values[n : n + 1], (SUBS, LANES))


def group_rows(values, width):
    rows, lanes = values.shape
    member = iota((2 * SUBS, lanes), 1) // width
    parts = []
    for part in range(lanes // width):
        mask = (member == part).astype(F32).astype(BF16)
        parts.append(values * jnp.concatenate([mask] * (rows // (2 * SUBS)), 0))
    return jnp.concatenate(parts, 0)


def lost_share(rate):
    square = rate * rate
    series = 1.0 + square / 110.0
    for factor in (72.0, 42.0, 20.0, 6.0):
        series = 1.0 + square / factor * series
    small = 2.0 * jnp.exp(-rate) * rate * series
    return jnp.where(rate < 0.5, small, 1.0 - jnp.exp(-2.0 * rate))


def locate(tile, refs):
    for ref in refs:
        if tile < ref.shape[-1] // LANES:
            return ref, tile
        tile -= ref.shape[-1] // LANES


def part_kernel(first, product_ref, *refs):
    refs[-1][...] = product_ref[:, first : first + refs[-1].shape[1]]


def own_kernel(
    filter_ref, rate_ref, residue_ref, product_0, product_1,
    bands_ref, lower_ref, conv_ref, taps_ref, fade_ref, weights_ref,
):
    groups, taps = filter_ref.shape
    channels = rate_ref.shape[1]
    width = channels // groups
    per_tile = LANES // width
    row, lane = iota((taps, taps), 0), iota((taps, taps), 1)
    flip = ((row + lane) % taps == 0).astype(BF16)
    flipped = jnp.dot(filter_ref[...], flip, preferred_element_type=F32)
    earlier = lane > row
    middle = taps // 2
    block = iota((SUBS, LANES), 0)
    for tile in range(channels // LANES):
        cols = tile_cols(tile)
        bands, tops = [], []
        for part in range(per_tile):
            group = tile * per_tile + part
            one = jnp.broadcast_to(flipped[group : group + 1], (taps, taps))
            circulant = pltpu.roll(one, 0, 1, stride=1, stride_axis=0)
            band = jnp.where(earlier, circulant, 0.0)
            bands_ref[tile, :, tile_cols(part)] = band[:middle].astype(BF16)
            if part % 2 == 0:
                turned = pltpu.roll(one, middle, 1, stride=1, stride_axis=0)[middle:]
                left = jnp.where(lane[:middle] > row[:middle], turned, 0.0)
            else:
                pair = jnp.where(lane[:middle] < middle, left, band[middle:])
                lower_ref[tile, :, tile_cols(part // 2)] = pair.astype(BF16)
            own = jnp.where(earlier, 0.0, circulant)
            bands.append(own[middle:].astype(BF16))
            if part % 2 == 0:
                near = own[:middle]
            else:
                turned = pltpu.roll(one, middle, 1, stride=1, stride_axis=0)[:middle]
                right = jnp.where(lane[:middle] - middle <= row[:middle], turned, 0.0)
                tops.append(jnp.where(lane[:middle] < middle, near, right).astype(BF16))
        product_ref, place = locate(tile, (product_0, product_1))
        product = product_ref[:, tile_cols(place)]
        conv_ref[:middle, cols] = jnp.dot(
            jnp.concatenate(tops, 1), group_rows(product[:middle], width), preferred_element_type=F32
        )
        conv_ref[middle:, cols] = jnp.dot(
            jnp.concatenate(bands, 1), group_rows(product, width), preferred_element_type=F32
        )
        rate = rate_ref[:, cols]
        gain = residue_ref[:, cols] * jnp.sqrt(lost_share(rate))
        fade = rate * -float(STEP)
        fade_ref[:, cols] = fade
        decay = jnp.exp(fade / STEP)
        powers = gain
        for lag in range(STEP):
            taps_ref[lag : lag + 1, cols] = jnp.sum(powers, 0, keepdims=True)
            powers = powers * decay
        jumps = [jnp.exp(fade * k) for k in JUMPS]
        start = gain * decay
        for n in range(gain.shape[0]):
            weights_ref[0, n, :, cols] = spread_row(decay, n)
            for k, jump in zip(JUMPS, jumps):
                place = JUMPS.index(k) + 1
                weights_ref[place, n, :, cols] = jnp.where(block >= k, spread_row(jump, n), 0.0)
            begin = spread_row(start, n)
            weights_ref[4, n, :, cols] = jnp.where(block >= 1, begin, 0.0)
            reach = jnp.exp(block.astype(F32) * spread_row(fade, n))
            weights_ref[5, n, :, cols] = begin * reach


def medium_kernel(
    start, halo_ref, bands_ref, lower_ref, conv_ref, query_ref, key_ref, weights_ref, *refs
):
    *others, out_mr_ref, source_ref, starts_ref, state_ref = refs
    poles = weights_ref.shape[1]
    width = LANES * LANES // bands_ref.shape[2]
    states = [other[:, tile_cols(i)] for other in others for i in range(other.shape[1] // LANES)]
    for tile in range(halo_ref.shape[1] // LANES):
        whole = start + tile
        cols, here = tile_cols(whole), tile_cols(tile)
        upper = jnp.dot(
            bands_ref[whole], group_rows(halo_ref[:, here], width), preferred_element_type=F32
        )
        later = halo_ref[bands_ref.shape[1] :, here]
        lower = jnp.dot(lower_ref[whole], group_rows(later, width), preferred_element_type=F32)
        conv = conv_ref[:, cols] + jnp.concatenate([upper, lower], 0)
        out_mr = (query_ref[:, cols].astype(F32) * conv).astype(BF16)
        out_mr_ref[:, here] = out_mr
        source_ref[tile] = key_ref[:, cols].astype(F32) * out_mr.astype(F32)
        rows = [source_ref[tile, strided(i), :] for i in range(STEP)]
        last = []
        for first in range(0, poles, MODES):
            modes = range(first, min(first + MODES, poles))
            decays = [weights_ref[0, n, :, cols] for n in modes]
            ends = [rows[0]] * len(modes)
            for i in range(1, STEP):
                ends = [end * decay + rows[i] for end, decay in zip(ends, decays)]
            for place, k in enumerate(JUMPS):
                weights = [weights_ref[place + 1, n, :, cols] for n in modes]
                ends = [end + w * pltpu.roll(end, k, 0) for end, w in zip(ends, weights)]
            for n, end in zip(modes, ends):
                starts_ref[n, :, here] = weights_ref[4, n, :, cols] * pltpu.roll(end, 1, 0)
                last.append(end[SUBS - 1 :])
        states.append(jnp.concatenate(last, 0).astype(BF16))
    if not others:
        for tile, state in enumerate(states):
            state_ref[:, tile_cols(tile)] = state
        return
    half = state_ref.shape[2] // LANES
    for tile, state in enumerate(states):
        for to in range(tile // half, state_ref.shape[0], 2):
            state_ref[to, :, tile_cols(tile % half)] = state


def own_half(tile, half):
    start = lax.axis_index("core") * half + tile * LANES
    return pl.ds(pl.multiple_of(start, LANES), LANES)


def tree_sum(values):
    while len(values) > 1:
        values = [a + b for a, b in zip(values[::2], values[1::2])] + values[len(values) // 2 * 2 :]
    return values[0]


def scan_stack(stack_ref, cols, step):
    states = [jnp.zeros(step.shape, F32)]
    for j in range(stack_ref.shape[0]):
        states.append(states[-1] * step + stack_ref[j, :, cols].astype(F32))
    return states


def pick(states, position):
    chosen = states[0]
    for j in range(1, len(states)):
        chosen = jnp.where(position == j, states[j], chosen)
    return chosen


def row_kernel(tokens, stack_ref, fade_ref, ahead_ref, spread_ref):
    half = stack_ref.shape[2]
    for tile in range(half // LANES):
        cols = tile_cols(tile)
        step = jnp.exp(fade_ref[:, own_half(tile, half)] * (tokens // STEP))
        states = scan_stack(stack_ref, cols, step)
        for core in range(2):
            ahead_ref[core, :, cols] = pick(states[core:-1:2], lax.axis_index("x"))
        state = states[-1].astype(BF16)
        for to in range(spread_ref.shape[0]):
            spread_ref[to, :, cols] = state


def join_kernel(tokens, stack_ref, ahead_ref, fade_ref, incoming_ref):
    half = stack_ref.shape[2]
    in_row = lax.axis_size("x") * 2
    first = (lax.axis_index("x") * 2).astype(F32)
    for tile in range(half // LANES):
        cols = tile_cols(tile)
        fade = fade_ref[:, own_half(tile, half)] * (tokens // STEP)
        states = scan_stack(stack_ref, cols, jnp.exp(fade * in_row))
        above = pick(states[:-1], lax.axis_index("y"))
        for core in range(2):
            reach = jnp.exp(fade * (first + core))
            incoming_ref[core, :, cols] = ahead_ref[core, :, cols] + reach * above


def long_kernel(
    incoming_ref, taps_ref, weights_ref, hidden_ref, query_ref, norm_ref,
    out_mr_0, source_0, starts_0, out_mr_1, source_1, starts_1,
    scaled_ref, squares_ref, conv_ref,
):
    tokens, channels = hidden_ref.shape
    poles, half = incoming_ref.shape[2:]
    core = lax.axis_index("core")
    squares = jnp.zeros((tokens, LANES), F32)
    for tile in range(channels // LANES):
        cols = tile_cols(tile)
        out_mr_ref, place = locate(tile, (out_mr_0, out_mr_1))
        source_ref, starts_ref = (source_0, starts_0) if out_mr_ref is out_mr_0 else (source_1, starts_1)
        here = tile_cols(place)
        side = tile * LANES // half
        incoming = incoming_ref[side, core, :, tile_cols(tile % (half // LANES))]
        rows = [source_ref[place, strided(i), :] for i in range(STEP)]
        sums = [jnp.zeros((SUBS, LANES), F32)] * STEP
        for lag in range(STEP):
            tap = jnp.broadcast_to(taps_ref[lag : lag + 1, cols], (SUBS, LANES))
            for i in range(lag, STEP):
                sums[i] = sums[i] + tap * rows[i - lag]
        for first in range(0, poles, MODES):
            modes = range(first, min(first + MODES, poles))
            decays = [weights_ref[0, n, :, cols] for n in modes]
            values = [
                starts_ref[n, :, here] + weights_ref[5, n, :, cols] * spread_row(incoming, n)
                for n in modes
            ]
            for i in range(STEP):
                if i:
                    values = [value * decay for value, decay in zip(values, decays)]
                sums[i] = sums[i] + tree_sum(values)
        for i in range(STEP):
            conv_ref[strided(i), :] = sums[i]
        combined = (
            hidden_ref[:, cols].astype(F32)
            + out_mr_ref[:, here].astype(F32)
            + query_ref[:, cols].astype(F32) * conv_ref[...]
        )
        scaled_ref[:, cols] = combined * norm_ref[:, cols]
        squares = squares + combined * combined
    total = jnp.sum(squares.T, 0, keepdims=True)
    squares_ref[...] = jnp.broadcast_to(total, squares_ref.shape)


def norm_kernel(total, scaled_ref, squares_ref, out_ref):
    tokens, channels = scaled_ref.shape
    square = jnp.sum(squares_ref[...], 0, keepdims=True)
    inverse = jnp.broadcast_to(lax.rsqrt(square / total + 1e-06), (tokens, tokens)).T
    for tile in range(channels // LANES):
        cols = tile_cols(tile)
        out_ref[:, cols] = (scaled_ref[:, cols] * inverse).astype(BF16)


def call(kernel, outs, scratch=(), cost=None):
    return pl.pallas_call(
        kernel,
        out_shape=[jax.ShapeDtypeStruct(shape, dtype) for shape, dtype in outs],
        scratch_shapes=[pltpu.VMEM(shape, dtype) for shape, dtype in scratch],
        compiler_params=pltpu.CompilerParams(vmem_limit_bytes=VMEM_LIMIT),
        cost_estimate=cost,
    )


def per_device(
    hidden_in,
    query_mr,
    key_mr,
    value_mr,
    query_li,
    key_li,
    mr_filter,
    li_rate,
    li_residue,
    norm_gain,
):
    tokens, channels = key_mr.shape
    filter_len, groups = mr_filter.shape
    poles = li_rate.shape[0]
    tiles = channels // LANES
    half = channels // 2
    ys = lax.axis_size("y")
    in_row = lax.axis_size("x") * lax.axis_size("core")
    long_op = pl.CostEstimate(
        flops=16 * groups * filter_len * filter_len * LANES, bytes_accessed=2**22, transcendentals=0
    )
    product = (key_mr.astype(F32) * value_mr.astype(F32)).astype(BF16)
    route = [(i, i + 1) for i in range(ys * in_row - 1)]
    cut = tiles * 5 // 8
    sizes = ((0, cut), (cut, tiles - cut))
    parts = []
    for first, size in sizes:
        parts += call(
            lambda *refs, first=first: part_kernel(first * LANES, *refs),
            [((tokens, size * LANES), BF16)],
            cost=long_op,
        )(product, *parts)
    halos = [lax.ppermute(part, SEQ, route) for part in parts]
    bands, lower, own, taps, fade, weights = call(
        own_kernel,
        [
            ((tiles, filter_len // 2, filter_len * groups // tiles), BF16),
            ((tiles, filter_len // 2, filter_len // 2 * groups // tiles), BF16),
            ((tokens, channels), F32),
            ((STEP, channels), F32),
            ((poles, channels), F32),
            ((6, poles, SUBS, channels), F32),
        ],
        cost=long_op,
    )(mr_filter.T, li_rate, li_residue, *parts)
    done, states = [], []
    for (first, size), halo in zip(sizes, halos):
        last = first + size == tiles
        *mixed, state = call(
            lambda *refs, first=first: medium_kernel(first, *refs),
            [
                ((tokens, size * LANES), BF16),
                ((size, tokens, LANES), F32),
                ((poles, SUBS, size * LANES), F32),
                ((in_row, poles, half) if last else (poles, size * LANES), BF16),
            ],
        )(halo, bands, lower, own, query_mr, key_li, weights, *states)
        done += mixed
        states = [state]
    (states,) = states
    states = lax.all_to_all(states, ("x", "core"), 0, 0, tiled=True)
    ahead, rows = call(
        lambda *refs: row_kernel(tokens, *refs),
        [((2, poles, half), F32), ((ys, poles, half), BF16)],
    )(states, fade)
    rows = lax.all_to_all(rows, "y", 0, 0, tiled=True)
    (incoming,) = call(lambda *refs: join_kernel(tokens, *refs), [((2, poles, half), F32)])(
        rows, ahead, fade
    )
    incoming = lax.all_gather(incoming, "core")
    scaled, squares = call(
        long_kernel,
        [((tokens, channels), F32), ((SUBS, tokens), F32)],
        [((tokens, LANES), F32)],
    )(
        incoming, taps, weights, hidden_in, query_li, norm_gain.reshape(1, channels), *done
    )
    chans = lax.axis_size("chan")
    squares = lax.all_to_all(squares.reshape(chans, 1, tokens), "chan", 0, 0, tiled=True)
    (out,) = call(
        lambda *refs: norm_kernel(channels * chans, *refs), [((tokens, channels), BF16)]
    )(scaled, squares.reshape(chans, tokens))
    return out


def solution(mesh):
    seq, chan = mesh.devices.shape
    xs = 4 if seq >= 64 else 2
    fine = Mesh(mesh.devices.reshape(seq // (2 * xs), xs, 2, chan), ("y", "x", "core", "chan"))
    both = P(SEQ, "chan")
    last = P(None, "chan")
    return jax.shard_map(
        per_device,
        mesh=fine,
        in_specs=(both,) * 6 + (last,) * 3 + (P("chan"),),
        out_specs=both,
        check_vma=False,
    )
```
